512 devices in a mesh: pool: 2 (over y_lo), wide: 64 (over z, x, core), narrow: 4 (over y_hi).
Axes of the slice: x: 4, y: 8 (y_hi: 4, y_lo: 2; y = y_hi * 2 + y_lo), z: 8, core: 2. Of those that a mesh axis runs over, the one named last changes fastest.
Arguments:
- queries: bfloat16 [128, 64, 128], P('wide', 'narrow'), may hold values from -160 to 160
- new_keys: bfloat16 [128, 4, 128], P('wide', 'narrow'), may hold values from -6 to 6
- new_values: bfloat16 [128, 4, 128], P('wide', 'narrow'), may hold values from -6 to 6
- key_cache: bfloat16 [128, 512, 4, 128], P('wide', None, 'narrow'), may hold values from -6 to 6
- value_cache: bfloat16 [128, 512, 4, 128], P('wide', None, 'narrow'), may hold values from -6 to 6
- lengths: int32 [128], P('wide'), may hold values from 8 to 512, as said below
- residual: bfloat16 [128, 2048], P(None, 'wide'), may hold values from -3 to 3
- out_weight: bfloat16 [2048, 8192], P('wide', 'narrow'), may hold values from -0.125 to 0.125
- norm_gain: bfloat16 [2048], replicated, may hold values from 0.099609375 to 1.8984375
- expert_ids: int32 [128, 8], replicated, may hold values from 0 to 63, all different within a row; in each aligned block of 128 rows (0 to 127, 128 to 255, ...) at most 32 rows name the same one
- expert_weights: float32 [128, 8], replicated, may hold values from 0.05 to 1
- gate_proj: bfloat16 [64, 768, 2048], P('wide', 'narrow'), may hold values from -0.125 to 0.125
- up_proj: bfloat16 [64, 768, 2048], P('wide', 'narrow'), may hold values from -0.125 to 0.125
- down_proj: bfloat16 [64, 768, 2048], P('wide', 'narrow'), may hold values from -0.3125 to 0.3125
Outputs:
- mixed: bfloat16 [128, 2048], P(('pool', 'narrow'), 'wide')
The draws below stay inside these ranges and needn't reach their ends.
Inputs may be any that keep to these rules, and one draw needn't show every extreme that they name: `lengths`: at least one row has all 512 slots filled. `expert_ids`: the 8 experts of a row differ. Over all 128 rows no expert is named by more than 32 rows, a bound that some block reaches.
All inputs are finite; a program needn't handle non-finite values.
Results may differ from the reference program's by a relative error of at most 0.018.
Values may be sent and summed in bfloat16 or wider, within the bound.
A program may use at most 64 MiB of HBM per device.

```python
import math
import jax
import jax.numpy as jnp
import numpy as np
from jax import lax

D = 2048
QH = 64
KVH = 4
HD = 128
EXP_FF = 768
CACHE = 512
ROWS = 128
EXPERTS = 64
TOPK = 8
GROUP = 16
FF_SLICE = 192
CAP = 32


def shared_keys(key):
    return jnp.clip(jax.random.normal(key, (ROWS, CACHE, KVH, HD), jnp.float32), -6.0, 6.0)


def draw_key_cache(key, part):
    base = shared_keys(key)
    return base.astype(jnp.bfloat16)


def draw_queries(key, part):
    key = jax.random.fold_in(key, 11)
    values = jax.random.normal(key, (ROWS, QH, HD), jnp.float32)
    return values.astype(jnp.bfloat16)


def draw_lengths(key, part):
    key = jax.random.fold_in(key, 5)
    first, second, third = jax.random.split(key, 3)
    raw = jax.random.randint(first, (ROWS,), 8, CACHE + 1)
    shifts = jax.random.randint(second, (ROWS,), 0, 4)
    filled = jnp.maximum(jnp.right_shift(raw, shifts), 8)
    chosen = jax.random.randint(third, (), 0, ROWS)
    return jnp.where(jnp.arange(ROWS) == chosen, CACHE, filled).astype(jnp.int32)


def level_of(key, dims, cuts, low, largest):
    gain, own = 1.0, jax.random.fold_in(key, 6)
    for axis_at, shards_of in cuts:
        steps = jnp.exp(jax.random.uniform(jax.random.fold_in(own, axis_at), (shards_of,), jnp.float32, low / len(cuts), largest / len(cuts)))
        gain = gain * jnp.repeat(steps, dims[axis_at] // shards_of).reshape([-1 if axis == axis_at else 1 for axis in range(len(dims))])
    return gain


def routed_block(rng, own, number, rows, count, top, reach, skew):
    order = jax.random.permutation(rng, count)
    crowded, ordinary = load_shares(count, rows * top, reach, skew, True), load_shares(count, rows * top, reach, skew, False)
    places = jnp.arange(count)

    def named(sizes, turn):
        used = int((sizes > 0).sum())
        fixed = max(1, used // 4)
        shifted = fixed + (places - fixed + turn * (used - fixed)) % max(1, count - fixed)
        return jnp.zeros((count,), jnp.int32).at[order[jnp.where(places < fixed, places, shifted)]].set(jnp.asarray(sizes, jnp.int32))

    sizes = jnp.where(number % 4 == 0, named(crowded, number // 4), named(ordinary, number - number // 4 - 1))
    mixed = jax.random.permutation(jax.random.fold_in(own, 3), count)
    donor, receiver = mixed[0:count // 2 * 2:2], mixed[1:count // 2 * 2:2]
    slack = jnp.minimum(sizes[donor] - 1, reach - sizes[receiver]) // 2
    slack = jnp.where((donor == order[0]) | (receiver == order[0]) | (sizes[receiver] == 0), 0, jnp.maximum(slack, 0))
    shifted = jax.random.randint(jax.random.fold_in(own, 4), (count // 2,), 0, 1 << 20) % (slack + 1)
    sizes = sizes.at[donor].add(-shifted).at[receiver].add(shifted)
    members = jnp.searchsorted(jnp.cumsum(sizes), jnp.arange(rows * top), side="right").astype(jnp.int32)
    grid = members.reshape(top, rows).T
    grid = grid[jax.random.permutation(jax.random.fold_in(own, 1), rows)]
    turn = jax.random.randint(jax.random.fold_in(own, 2), (rows, 1), 0, top)
    return jnp.take_along_axis(grid, (jnp.arange(top)[None, :] + turn) % top, axis=1)


def load_shares(amount, total, bound, skew, full):
    weights = [(1 << 20) // math.isqrt(grade ** skew) + 1 for grade in range(1, amount + 1)]
    largest = bound if full else min(bound, max(-(-total // amount), total * weights[0] // sum(weights)))
    least = 1 if total - largest >= amount - 1 else 0
    given, surplus = [largest] + [least] * (amount - 1), total - largest - least * (amount - 1)
    while surplus > 0:
        movable = [i for i in range(1, amount) if given[i] < largest] or [i for i in range(1, amount) if given[i] < bound]
        whole, remaining = sum([weights[i] for i in movable]), surplus
        for i in movable:
            extra = min(bound - given[i], max(1, remaining * weights[i] // whole), surplus)
            given[i] = given[i] + extra
            surplus = surplus - extra
    return np.array(given)


def gaussian(own_key, extent, scale, reach, shards=(), held_as=jnp.bfloat16):
    array = jax.random.normal(own_key, extent, jnp.float32) * scale
    if len(shards) > 0:
        array = level_of(own_key, extent, shards, -0.22, 0.18) * array
    return jnp.clip(array, min=-reach, max=reach).astype(held_as)


def setup_inputs(seed: int = 0) -> dict:
    seeds = jax.random.split(jax.random.key(seed), 15)
    queries = draw_queries(jax.random.fold_in(seeds[14], 71), 0)
    new_keys = gaussian(seeds[1], (ROWS, KVH, HD), 1.0, 6.0, ((0, 64), (1, 4)))
    new_values = gaussian(seeds[2], (ROWS, KVH, HD), 1.0, 6.0, ((0, 64), (1, 4)))
    key_cache = draw_key_cache(jax.random.fold_in(seeds[14], 71), 0)
    value_cache = gaussian(seeds[4], (ROWS, CACHE, KVH, HD), 1.0, 6.0, ((0, 64), (2, 4)))
    lengths = draw_lengths(jax.random.fold_in(seeds[14], 71), 0)
    residual = gaussian(seeds[6], (ROWS, D), 0.5, 3.0, ((1, 64),))
    out_weight = gaussian(seeds[7], (D, QH * HD), (QH * HD // 4) ** -0.5, 0.125, ((0, 64), (1, 4)))
    norm_gain = jnp.clip(1.0 + 0.18 * jax.random.normal(seeds[8], (D,), jnp.float32), 0.099609375, 1.8984375).astype(jnp.bfloat16)
    expert_ids_keys = jax.random.split(jax.random.fold_in(seeds[9], 1), ROWS // ROWS)
    expert_ids_turns = jax.random.permutation(jax.random.fold_in(seeds[9], 3), ROWS // ROWS)
    expert_ids = jax.vmap(lambda own, number: routed_block(jax.random.fold_in(seeds[9], 2), own, number, ROWS, EXPERTS, TOPK, CAP, 2))(expert_ids_keys, expert_ids_turns).reshape((ROWS, TOPK))
    expert_weights = jnp.clip(jnp.exp(jax.random.uniform(seeds[10], (ROWS, TOPK), jnp.float32, math.log(0.05), math.log(1.0))), 0.05, 1.0)
    gate_proj = gaussian(seeds[11], (EXPERTS, EXP_FF, D), D ** -0.5, 0.125, ((0, 64), (1, 4)))
    up_proj = gaussian(seeds[12], (EXPERTS, EXP_FF, D), D ** -0.5, 0.125, ((0, 64), (1, 4)))
    down_proj = gaussian(seeds[13], (EXPERTS, EXP_FF, D), (EXP_FF // 2) ** -0.5, 0.3125, ((0, 64), (1, 4)))
    return dict(queries=queries, new_keys=new_keys, new_values=new_values, key_cache=key_cache, value_cache=value_cache, lengths=lengths, residual=residual, out_weight=out_weight, norm_gain=norm_gain, expert_ids=expert_ids, expert_weights=expert_weights, gate_proj=gate_proj, up_proj=up_proj, down_proj=down_proj)


def attend_row(items):
    query, new_key, new_value, keys, values, length = items
    scale = 1.0 / HD ** 0.5
    query = query.astype(jnp.float32).reshape(KVH, GROUP, HD)
    scores = jnp.einsum('kgd,ckd->kgc', query, keys.astype(jnp.float32)) * scale
    self_score = jnp.einsum('kgd,kd->kg', query, new_key.astype(jnp.float32)) * scale
    valid = (jnp.arange(CACHE, dtype=jnp.int32) < length)[None, None, :]
    scores = jnp.where(valid, scores, -1e+30)
    peak = jnp.maximum(lax.optimization_barrier(jnp.max(scores, axis=-1)), self_score)
    weights = jnp.where(valid, jnp.exp(scores - peak[..., None]), 0.0)
    self_weight = jnp.exp(self_score - peak)
    total = lax.optimization_barrier(jnp.sum(weights, axis=-1)) + self_weight
    probs = lax.optimization_barrier((weights / total[..., None]).astype(jnp.bfloat16)).astype(jnp.float32)
    self_prob = lax.optimization_barrier((self_weight / total).astype(jnp.bfloat16)).astype(jnp.float32)
    mixed = jnp.einsum('kgc,ckd->kgd', probs, values.astype(jnp.float32))
    mixed = mixed + self_prob[..., None] * new_value.astype(jnp.float32)[:, None, :]
    return mixed.astype(jnp.bfloat16).reshape(QH * HD)

def reference(queries, new_keys, new_values, key_cache, value_cache, lengths, residual, out_weight, norm_gain, expert_ids, expert_weights, gate_proj, up_proj, down_proj):
    heads_out = lax.map(attend_row, (queries, new_keys, new_values, key_cache, value_cache, lengths))
    span = GROUP * HD
    hidden = residual.astype(jnp.float32)
    for group in range(KVH):
        piece = jnp.dot(heads_out[:, group * span:(group + 1) * span], out_weight[:, group * span:(group + 1) * span].T, preferred_element_type=jnp.float32)
        hidden = hidden + lax.optimization_barrier(piece.astype(jnp.bfloat16)).astype(jnp.float32)
    normed = (hidden * lax.rsqrt(lax.optimization_barrier(jnp.mean(hidden * hidden, axis=-1, keepdims=True)) + 1e-06) * norm_gain.astype(jnp.float32)).astype(jnp.bfloat16)
    shares = expert_weights / lax.optimization_barrier(jnp.sum(expert_weights, axis=-1, keepdims=True))
    slot_range = jnp.arange(CAP, dtype=jnp.int32)

    def expert_step(carry, expert):
        hit = expert_ids == expert
        row_hit = lax.optimization_barrier(jnp.sum(hit.astype(jnp.int32), axis=-1)).astype(jnp.int32)
        row_share = lax.optimization_barrier(jnp.sum(jnp.where(hit, shares, 0.0), axis=-1))
        slot = (jnp.cumsum(row_hit) - 1).astype(jnp.int32)
        select = jnp.where((slot[None, :] == slot_range[:, None]) & (row_hit[None, :] > 0), 1.0, 0.0).astype(jnp.float32)
        rows_in = jnp.dot(select, normed.astype(jnp.float32), precision=lax.Precision.HIGHEST).astype(jnp.bfloat16)
        slot_share = jnp.dot(select, row_share, precision=lax.Precision.HIGHEST)
        gate_vals = jnp.dot(rows_in, gate_proj[expert].T, preferred_element_type=jnp.float32)
        up_vals = jnp.dot(rows_in, up_proj[expert].T, preferred_element_type=jnp.float32)
        activated = (jax.nn.silu(gate_vals) * up_vals).astype(jnp.bfloat16)
        total = jnp.zeros((CAP, D), jnp.float32)
        for slice_index in range(EXP_FF // FF_SLICE):
            start = slice_index * FF_SLICE
            term = jnp.dot(activated[:, start:start + FF_SLICE], down_proj[expert, start:start + FF_SLICE], preferred_element_type=jnp.float32)
            total = total + lax.optimization_barrier((term * slot_share[:, None]).astype(jnp.bfloat16)).astype(jnp.float32)
        return (carry + jnp.dot(select.T, total, precision=lax.Precision.HIGHEST), None)
    moe, unused = lax.scan(expert_step, jnp.zeros((ROWS, D), jnp.float32), jnp.arange(EXPERTS, dtype=jnp.int32))
    return (hidden + moe).astype(jnp.bfloat16)
```

```python
import functools

import jax
import jax.numpy as jnp
from jax import lax
from jax.experimental import pallas as pl
from jax.experimental.pallas import tpu as pltpu
from jax.sharding import PartitionSpec as P

BF16, F32 = jnp.bfloat16, jnp.float32
NT = (((1,), (1,)), ((), ()))
HIGH = lax.Precision.HIGHEST


def iota(shape, axis):
    return lax.broadcasted_iota(jnp.int32, shape, axis)


def ones_where(mask, dtype=BF16):
    return jnp.where(mask, 1.0, 0.0).astype(dtype)


def send(src, dst, send_sem, recv_sem, device):
    pltpu.make_async_remote_copy(
        src_ref=src,
        dst_ref=dst,
        send_sem=send_sem,
        recv_sem=recv_sem,
        device_id=device,
        device_id_type=pl.DeviceIdType.MESH,
    ).start()


def wait_bytes(ref, sem):
    pltpu.make_async_copy(ref, ref, sem).wait()


def step(
    q_h, nk_h, nv_h, k_h, v_h, len_h, res_h, w_h, gain_h, ids_h, ew_h, gate_h, up_h, down_h,
    out_ref,
    q_v, nk_v, nv_v, k_v, v_v, len_v, res_v, w_v, gain_v, ids_v, ew_v, gate_v, up_v, down_v,
    heads, heads_f, parts, hidden, gu_w, down_w, made, summed, partial, by_z, final,
    load_sem, send_sem, recv_sem,
):
    p = lax.axis_index("pool")
    w = lax.axis_index("wide")
    n = lax.axis_index("narrow")
    z, xc = w // 8, w % 8
    pn = p * 4 + n

    loads = [
        (q_h.at[p], q_v), (k_h.at[p], k_v), (len_h, len_v), (nk_h, nk_v), (nv_h, nv_v), (v_h.at[p], v_v),
        (w_h, w_v), (res_h, res_v), (gain_h, gain_v), (ids_h, ids_v), (ew_h, ew_v),
        (gate_h, gate_v), (up_h, up_v), (down_h, down_v),
    ]
    loads = [pltpu.make_async_copy(s, d, load_sem.at[i]) for i, (s, d) in enumerate(loads)]
    for copy in loads:
        copy.start()

    z_peers = [{"wide": (z + d) % 8 * 8 + xc} for d in range(1, 8)]
    xc_peers = [{"wide": z * 8 + (xc + d) % 8} for d in range(1, 8)]
    n_peers = [{"narrow": (n + d) % 4} for d in range(1, 4)]
    pn_peers = [{"pool": (pn + d) % 8 // 4, "narrow": (pn + d) % 4} for d in range(1, 8)]

    barrier = pltpu.get_barrier_semaphore()
    peers = z_peers + xc_peers + pn_peers
    for peer in peers:
        pl.semaphore_signal(barrier, inc=1, device_id=peer, device_id_type=pl.DeviceIdType.MESH)

    for copy in loads[:6]:
        copy.wait()
    q = q_v[...]
    scale = 128.0**-0.5
    scores = lax.dot_general(q, k_v[...], NT, preferred_element_type=F32) * scale
    nk = jnp.where(p == 0, nk_v[0:1].astype(F32), nk_v[1:2].astype(F32))
    nv = jnp.where(p == 0, nv_v[0:1].astype(F32), nv_v[1:2].astype(F32))
    self_score = jnp.sum(q.astype(F32) * nk, axis=1, keepdims=True) * scale
    valid = iota((16, 512), 1) < len_v[p]
    scores = jnp.where(valid, scores, -1e30)
    peak = jnp.maximum(jnp.max(scores, axis=1, keepdims=True), self_score)
    weights = jnp.where(valid, jnp.exp(scores - peak), 0.0)
    self_weight = jnp.exp(self_score - peak)
    total = jnp.sum(weights, axis=1, keepdims=True) + self_weight
    probs = (weights / total).astype(BF16)
    self_prob = (self_weight / total).astype(BF16).astype(F32)
    mixed = jnp.dot(probs, v_v[...], preferred_element_type=F32) + self_prob * nv
    heads[z, xc] = mixed.astype(BF16)

    def spread_z(buf, phase):
        mine = buf.at[z, xc]
        for peer in z_peers:
            send(mine, mine, send_sem.at[phase], recv_sem.at[phase], peer)

    def spread_xc(buf, phase):
        wait_bytes(buf.at[pl.ds(0, 7), 0], recv_sem.at[phase - 1])
        mine = buf.at[:, xc]
        for peer in xc_peers:
            send(mine, mine, send_sem.at[phase], recv_sem.at[phase], peer)

    def arrive_xc(buf, phase):
        wait_bytes(buf.at[:, pl.ds(0, 7)], recv_sem.at[phase])

    pl.semaphore_wait(barrier, len(peers))
    spread_z(heads, 0)

    for copy in loads[6:]:
        copy.wait()
    gain = gain_v[...].reshape(1, 2048).astype(F32)
    src, dst = iota((256, 256), 0), iota((256, 256), 1)
    perm = ones_where(dst == (src % 32 // 16) * 128 + src // 32 * 16 + src % 16)
    for i, ref in enumerate((gate_v, up_v)):
        for b in range(8):
            cols = slice(b * 256, (b + 1) * 256)
            scaled = (ref[:, cols].astype(F32) * gain[:, cols]).astype(BF16)
            moved = jnp.dot(scaled, perm, preferred_element_type=F32).astype(BF16)
            gu_w[i * 192 : (i + 1) * 192, b * 128 : (b + 1) * 128] = moved[:, :128]
            gu_w[384 + i * 192 : 384 + (i + 1) * 192, b * 128 : (b + 1) * 128] = moved[:, 128:]

    spread_xc(heads, 1)

    perm_t = ones_where(src == (dst % 32 // 16) * 128 + dst // 32 * 16 + dst % 16)
    for b in range(8):
        block = down_v[:, b * 256 : (b + 1) * 256]
        moved = lax.dot_general(perm_t, block, NT, preferred_element_type=F32).astype(BF16)
        down_w[0, b * 128 : (b + 1) * 128] = moved[:128]
        down_w[1, b * 128 : (b + 1) * 128] = moved[128:]
    row, lane = iota((128, 128), 0), iota((128, 128), 1)
    pick_low = (lane < 64) & (row == 2 * lane + p)
    pick_high = (lane >= 64) & (row == 2 * (lane - 64) + p)
    res = res_v[...]
    own_res = jnp.dot(res[0:16], ones_where(pick_low), preferred_element_type=F32) + jnp.dot(
        res[16:32], ones_where(pick_high), preferred_element_type=F32
    )
    ew = ew_v[...]
    share = jnp.sum(jnp.where(ids_v[...] == w, ew, 0.0), axis=0, keepdims=True)
    share = share / jnp.sum(ew, axis=0, keepdims=True)
    share = jnp.dot(
        jnp.broadcast_to(share, (8, 128)), ones_where(pick_low, F32), precision=HIGH, preferred_element_type=F32
    )[0:1]
    out_row, out_lane = iota((16, 128), 0), iota((16, 128), 1)
    first = pn * 16
    out_res = lax.dot_general(ones_where(out_lane == first + out_row), res, NT, preferred_element_type=F32)

    arrive_xc(heads, 1)
    heads_f[...] = heads[...].reshape(1024, 128).astype(F32)
    rows = jnp.concatenate([heads_f[pl.ds(g, 64, stride=16), :].astype(BF16) for g in range(16)], axis=1)
    part = lax.dot_general(w_v[...], rows, NT, preferred_element_type=F32)
    part = jnp.concatenate([part[0:16], part[16:32]], axis=1).astype(BF16)

    parts[n] = part
    for peer in n_peers:
        send(parts.at[n], parts.at[n], send_sem.at[2], recv_sem.at[2], peer)
    wait_bytes(parts.at[pl.ds(0, 3)], recv_sem.at[2])
    own = own_res
    for i in range(4):
        own = own + parts[i].astype(F32)
    hidden[z, xc] = own.astype(BF16)
    spread_z(hidden, 3)
    spread_xc(hidden, 4)
    arrive_xc(hidden, 4)

    hid = hidden[...].reshape(1024, 128)
    both = jnp.dot(gu_w[...], hid, preferred_element_type=F32)
    hid_f = hid.astype(F32)
    square = jnp.sum(hid_f * hid_f, axis=0, keepdims=True)
    square = square + pltpu.roll(square, 64, 1)
    inv = lax.rsqrt(square * (1.0 / 2048) + 1e-6)
    both = (both[0:384] + pltpu.roll(both[384:768], 64, 1)) * inv
    gate_vals, up_vals = both[0:192], both[192:384]
    act = gate_vals / (1.0 + jnp.exp(-gate_vals)) * up_vals * share
    act_low, act_high = act.astype(BF16), pltpu.roll(act, 64, 1).astype(BF16)
    output = jnp.dot(down_w[0], act_low, preferred_element_type=F32) + jnp.dot(
        down_w[1], act_high, preferred_element_type=F32
    )
    made[...] = output.astype(BF16).reshape(8, 8, 16, 128)

    for d, peer in zip(range(1, 8), xc_peers):
        send(made.at[:, (xc + d) % 8], partial.at[xc], send_sem.at[5], recv_sem.at[5], peer)
    partial[xc] = made[:, xc]
    wait_bytes(partial.at[pl.ds(0, 7)], recv_sem.at[5])
    acc = partial[0].astype(F32)
    for i in range(1, 8):
        acc = acc + partial[i].astype(F32)
    summed[...] = acc.astype(BF16)
    for d, peer in zip(range(1, 8), z_peers):
        send(summed.at[(z + d) % 8], by_z.at[z], send_sem.at[6], recv_sem.at[6], peer)
    by_z[z] = summed[z]
    wait_bytes(by_z.at[pl.ds(0, 7)], recv_sem.at[6])
    acc = part.astype(F32)
    for i in range(8):
        acc = acc + by_z[i].astype(F32)
    final[pn] = acc.astype(BF16)
    for peer in pn_peers:
        send(final.at[pn], final.at[pn], send_sem.at[7], recv_sem.at[7], peer)
    wait_bytes(final.at[pl.ds(0, 7)], recv_sem.at[7])
    even, odd = final[0].astype(F32), final[4].astype(F32)
    for i in range(1, 4):
        even, odd = even + final[i].astype(F32), odd + final[4 + i].astype(F32)
    low = out_lane < 64
    table = jnp.concatenate(
        [jnp.where(low, even, pltpu.roll(odd, 64, 1)), jnp.where(low, pltpu.roll(even, 64, 1), odd)], axis=0
    )
    chosen = jnp.where(low, 2 * out_lane, 2 * (out_lane - 64) + 1) == first + out_row
    out = lax.dot_general(ones_where(chosen, F32), table, NT, precision=HIGH, preferred_element_type=F32)
    out_ref[...] = (out + out_res).astype(BF16)

    for phase, ref in (
        (0, heads.at[pl.ds(0, 7), 0]),
        (1, heads.at[:, pl.ds(0, 7)]),
        (2, parts.at[pl.ds(0, 3)]),
        (3, hidden.at[pl.ds(0, 7), 0]),
        (4, hidden.at[:, pl.ds(0, 7)]),
        (5, partial.at[pl.ds(0, 7)]),
        (6, by_z.at[pl.ds(0, 7)]),
        (7, final.at[pl.ds(0, 7)]),
    ):
        wait_bytes(ref, send_sem.at[phase])


def local(
    queries, new_keys, new_values, key_cache, value_cache, lengths, residual, out_weight, norm_gain,
    expert_ids, expert_weights, gate_proj, up_proj, down_proj,
):
    args = (
        queries, new_keys[:, 0, :], new_values[:, 0, :], key_cache[:, :, 0, :], value_cache[:, :, 0, :], lengths,
        residual.T, out_weight, norm_gain, expert_ids.T, expert_weights.T, gate_proj[0], up_proj[0], down_proj[0],
    )
    held = [pltpu.VMEM(a.shape, a.dtype) for a in args]
    for i in (0, 3, 4):
        held[i] = pltpu.VMEM(args[i].shape[1:], BF16)
    held[5] = pltpu.SMEM((2,), jnp.int32)
    tiles = lambda *lead: pltpu.VMEM((*lead, 16, 128), BF16)
    return pl.pallas_call(
        step,
        out_shape=jax.ShapeDtypeStruct((16, 32), BF16),
        in_specs=[pl.BlockSpec(memory_space=pl.ANY)] * len(args),
        out_specs=pl.BlockSpec(memory_space=pltpu.VMEM),
        scratch_shapes=held
        + [
            tiles(8, 8), pltpu.VMEM((1024, 128), F32), tiles(4), tiles(8, 8),
            pltpu.VMEM((768, 1024), BF16), pltpu.VMEM((2, 1024, 192), BF16),
            tiles(8, 8), tiles(8), tiles(8, 8), tiles(8), tiles(8),
            pltpu.SemaphoreType.DMA((14,)), pltpu.SemaphoreType.DMA((8,)), pltpu.SemaphoreType.DMA((8,)),
        ],
        compiler_params=pltpu.CompilerParams(
            collective_id=0, has_side_effects=True, vmem_limit_bytes=56 * 1024 * 1024
        ),
    )(*args)


def solution(mesh):
    in_specs = (
        P("wide", "narrow", None),
        P("wide", "narrow", None),
        P("wide", "narrow", None),
        P("wide", None, "narrow", None),
        P("wide", None, "narrow", None),
        P("wide"),
        P(None, "wide"),
        P("wide", "narrow"),
        P(),
        P(),
        P(),
        P("wide", "narrow", None),
        P("wide", "narrow", None),
        P("wide", "narrow", None),
    )
    return jax.shard_map(
        local, mesh=mesh, in_specs=in_specs, out_specs=P(("pool", "narrow"), "wide"), check_vma=False
    )
```

```python
import functools

import jax
import jax.numpy as jnp
from jax import lax
from jax.experimental import pallas as pl
from jax.experimental.pallas import tpu as pltpu
from jax.sharding import PartitionSpec as P

BF16, F32 = jnp.bfloat16, jnp.float32
NT = (((1,), (1,)), ((), ()))
HIGH = lax.Precision.HIGHEST


def iota(shape, axis):
    return lax.broadcasted_iota(jnp.int32, shape, axis)


def ones_where(mask, dtype=BF16):
    return jnp.where(mask, 1.0, 0.0).astype(dtype)


def send(src, dst, send_sem, recv_sem, device):
    pltpu.make_async_remote_copy(
        src_ref=src,
        dst_ref=dst,
        send_sem=send_sem,
        recv_sem=recv_sem,
        device_id=device,
        device_id_type=pl.DeviceIdType.MESH,
    ).start()


def wait_bytes(ref, sem):
    pltpu.make_async_copy(ref, ref, sem).wait()


FAR, NEAR = (4, 3, 5, 2, 6, 1, 7), (1, 7, 2, 6, 3, 5, 4)


def far_offset(i):
    return 4 + (2 * (i % 2) - 1) * ((i + 1) // 2)


def step(
    k_h, q_h, len_h, nk_h, nv_h, v_h, w_h, res_h, gain_h, ids_h, ew_h, gate_h, up_h, down_h,
    out_ref,
    k_v, q_v, len_v, nk_v, nv_v, v_v, w_v, res_v, gain_v, ids_v, ew_v, gate_v, up_v, down_v,
    heads, heads_f, parts, hidden, gu_w, down_w, both, made, partial, pieces, final,
    load_sem, send_sem, recv_sem,
):
    p = lax.axis_index("pool")
    w = lax.axis_index("wide")
    n = lax.axis_index("narrow")
    z, xc = w // 8, w % 8
    pn = p * 4 + n

    loads = [
        (k_h.at[p], k_v), (q_h.at[p], q_v), (len_h, len_v), (nk_h, nk_v), (nv_h, nv_v), (v_h.at[p], v_v),
        (w_h, w_v), (res_h, res_v), (gain_h, gain_v), (ids_h, ids_v), (ew_h, ew_v),
        (gate_h, gate_v), (up_h, up_v), (down_h, down_v),
    ]
    loads = [pltpu.make_async_copy(s, d, load_sem.at[i]) for i, (s, d) in enumerate(loads)]
    for copy in loads[:6]:
        copy.start()

    def at_z(dz):
        return (z + dz) % 8

    def wide_peer(dz, dxc):
        return {"wide": at_z(dz) * 8 + (xc + dxc) % 8}

    def zn_peer(dz, dn):
        return {"wide": at_z(dz) * 8 + xc, "narrow": (n + dn) % 4}

    def zpn_peer(dz, dpn):
        return {"pool": (pn + dpn) % 8 // 4, "wide": at_z(dz) * 8 + xc, "narrow": (pn + dpn) % 4}

    barrier = pltpu.get_barrier_semaphore()
    greeted = [wide_peer(d, 0) for d in FAR] + [zn_peer(0, d) for d in (2, 1, 3)]
    greeted += [wide_peer(0, d) for d in FAR] + [{"pool": 1 - p}]
    for peer in greeted:
        pl.semaphore_signal(barrier, inc=1, device_id=peer, device_id_type=pl.DeviceIdType.MESH)
    for copy in loads[6:]:
        copy.start()

    loads[0].wait()
    loads[1].wait()
    q = q_v[...]
    scale = 128.0**-0.5
    scores = lax.dot_general(q, k_v[...], NT, preferred_element_type=F32) * scale
    for copy in loads[2:6]:
        copy.wait()
    nk = jnp.where(p == 0, nk_v[0:1].astype(F32), nk_v[1:2].astype(F32))
    nv = jnp.where(p == 0, nv_v[0:1].astype(F32), nv_v[1:2].astype(F32))
    self_score = jnp.sum(q.astype(F32) * nk, axis=1, keepdims=True) * scale
    valid = iota((16, 512), 1) < len_v[p]
    scores = jnp.where(valid, scores, -1e30)
    peak = jnp.maximum(jnp.max(scores, axis=1, keepdims=True), self_score)
    weights = jnp.where(valid, jnp.exp(scores - peak), 0.0)
    self_weight = jnp.exp(self_score - peak)
    total = jnp.sum(weights, axis=1, keepdims=True) + self_weight
    probs = (weights / total).astype(BF16)
    self_prob = (self_weight / total).astype(BF16).astype(F32)
    mixed = jnp.dot(probs, v_v[...], preferred_element_type=F32) + self_prob * nv
    heads[z, xc] = mixed.astype(BF16)

    def fan_out(source, send_index, recv_index):
        @pl.loop(0, 7)
        def _(i):
            send(source, source, send_sem.at[send_index], recv_sem.at[recv_index], wide_peer(0, far_offset(i)))

    pl.semaphore_wait(barrier, len(greeted))
    for d in FAR:
        send(heads.at[z, xc], heads.at[z, xc], send_sem.at[0], recv_sem.at[d], wide_peer(d, 0))
    fan_out(heads.at[z, xc], 1, 0)

    for copy in loads[6:]:
        copy.wait()
    gain = gain_v[...].reshape(1, 2048).astype(F32)
    src, dst = iota((256, 256), 0), iota((256, 256), 1)
    perm = ones_where(dst == (src % 32 // 16) * 128 + src // 32 * 16 + src % 16)
    for i, ref in enumerate((gate_v, up_v)):
        for b in range(8):
            cols = slice(b * 256, (b + 1) * 256)
            scaled = (ref[:, cols].astype(F32) * gain[:, cols]).astype(BF16)
            moved = jnp.dot(scaled, perm, preferred_element_type=F32).astype(BF16)
            gu_w[i * 192 : (i + 1) * 192, b * 128 : (b + 1) * 128] = moved[:, :128]
            gu_w[384 + i * 192 : 384 + (i + 1) * 192, b * 128 : (b + 1) * 128] = moved[:, 128:]

    for d in NEAR:
        tile = heads.at[at_z(8 - d), xc]
        wait_bytes(tile, recv_sem.at[d])
        fan_out(tile, 1, 0)

    perm_t = ones_where(src == (dst % 32 // 16) * 128 + dst // 32 * 16 + dst % 16)
    for b in range(8):
        block = down_v[:, b * 256 : (b + 1) * 256]
        moved = lax.dot_general(perm_t, block, NT, preferred_element_type=F32).astype(BF16)
        down_w[0, b * 128 : (b + 1) * 128] = moved[:128]
        down_w[1, b * 128 : (b + 1) * 128] = moved[128:]
    row, lane = iota((128, 128), 0), iota((128, 128), 1)
    pick_low = (lane < 64) & (row == 2 * lane + p)
    pick_high = (lane >= 64) & (row == 2 * (lane - 64) + p)
    res = res_v[...]
    own_res = jnp.dot(res[0:16], ones_where(pick_low), preferred_element_type=F32) + jnp.dot(
        res[16:32], ones_where(pick_high), preferred_element_type=F32
    )
    own_res = jnp.where(n == 0, own_res, 0.0)
    ew = ew_v[...]
    share = jnp.sum(jnp.where(ids_v[...] == w, ew, 0.0), axis=0, keepdims=True)
    share = share / jnp.sum(ew, axis=0, keepdims=True)
    share = jnp.dot(
        jnp.broadcast_to(share, (8, 128)), ones_where(pick_low, F32), precision=HIGH, preferred_element_type=F32
    )[0:1]
    out_row, out_lane = iota((16, 128), 0), iota((16, 128), 1)
    out_res = lax.dot_general(ones_where(out_lane == pn * 16 + out_row), res, NT, preferred_element_type=F32)

    wait_bytes(heads.at[:, pl.ds(0, 7)], recv_sem.at[0])
    heads_f[...] = heads[...].reshape(1024, 128).astype(F32)
    rows = jnp.concatenate([heads_f[pl.ds(g, 64, stride=16), :].astype(BF16) for g in range(16)], axis=1)
    part = lax.dot_general(w_v[...], rows, NT, preferred_element_type=F32)
    part = jnp.concatenate([part[0:16], part[16:32]], axis=1).astype(BF16).astype(F32)

    parts[z * 4 + n] = (part + own_res).astype(BF16)
    for dn in (2, 1, 3, 0):
        for dz in FAR + (0,) if dn else FAR:
            send(parts.at[z * 4 + n], parts.at[z * 4 + n], send_sem.at[2], recv_sem.at[8 + dz], zn_peer(dz, dn))
    for dz in (0,) + NEAR:
        from_z = at_z(8 - dz)
        wait_bytes(parts.at[pl.ds(0, 4 if dz else 3)], recv_sem.at[8 + dz])
        hid = parts[from_z * 4].astype(F32)
        for i in range(1, 4):
            hid = hid + parts[from_z * 4 + i].astype(F32)
        hidden[from_z, xc] = hid.astype(BF16)
        fan_out(hidden.at[from_z, xc], 3, 16 + dz)

    square = jnp.zeros((1, 128), F32)
    for group in ((0,), (1, 7), (2, 6), (3, 5), (4,)):
        tiles, blocks = [], []
        for dz in group:
            from_z = at_z(8 - dz)
            wait_bytes(hidden.at[from_z, pl.ds(0, 7)], recv_sem.at[16 + dz])
            tiles.append(hidden[from_z].reshape(128, 128))
            blocks.append(gu_w[:, pl.ds(pl.multiple_of(from_z * 128, 128), 128)])
        tile = jnp.concatenate(tiles, axis=0)
        term = jnp.dot(jnp.concatenate(blocks, axis=1), tile, preferred_element_type=F32)
        both[...] = term if group == (0,) else both[...] + term
        tile = tile.astype(F32)
        square = square + jnp.sum(tile * tile, axis=0, keepdims=True)
    square = square + pltpu.roll(square, 64, 1)
    inv = lax.rsqrt(square * (1.0 / 2048) + 1e-6)
    act = (both[0:384] + pltpu.roll(both[384:768], 64, 1)) * inv
    gate_vals, up_vals = act[0:192], act[192:384]
    act = gate_vals / (1.0 + jnp.exp(-gate_vals)) * up_vals * share
    act_low, act_high = act.astype(BF16), pltpu.roll(act, 64, 1).astype(BF16)

    for dz in FAR + (0,):
        to_z = at_z(dz)
        rows_w = pl.ds(pl.multiple_of(to_z * 128, 128), 128)
        output = jnp.dot(down_w[0, rows_w], act_low, preferred_element_type=F32) + jnp.dot(
            down_w[1, rows_w], act_high, preferred_element_type=F32
        )
        made[to_z] = output.astype(BF16).reshape(8, 16, 128)

        @pl.loop(0, 7)
        def _(i):
            d = far_offset(i)
            send(
                made.at[to_z, (xc + d) % 8], partial.at[to_z, xc], send_sem.at[4], recv_sem.at[24 + dz],
                wide_peer(0, d),
            )

        partial[to_z, xc] = made[to_z, xc]

    low = out_lane < 64
    repeat = ones_where(iota((128, 16), 0) // 8 == iota((128, 16), 1))
    same_row = lane % 8 == row % 8
    piece_of = ones_where((out_lane // 64 == out_row % 2) & (out_lane % 64 // 8 == out_row // 2))
    for dz in FAR + (0,):
        to_z = at_z(dz)
        wait_bytes(partial.at[to_z, pl.ds(0, 7)], recv_sem.at[24 + dz])
        acc = partial[to_z, 0].astype(F32)
        for i in range(1, 8):
            acc = acc + partial[to_z, i].astype(F32)
        if dz == 0:
            acc = acc + part
        spread = jnp.dot(repeat, acc.astype(BF16), preferred_element_type=F32)
        spread = jnp.where(same_row, spread, 0.0).astype(BF16)
        piece = lax.dot_general(piece_of, spread, NT, preferred_element_type=F32)
        pieces[to_z] = piece.reshape(8, 2, 128)

        @pl.loop(0, 7)
        def _(i):
            d = far_offset(i)
            send(pieces.at[to_z, (pn + d) % 8], final.at[z * 8 + pn], send_sem.at[5], recv_sem.at[32], zpn_peer(dz, d))

        if dz:
            send(pieces.at[to_z, pn], final.at[z * 8 + pn], send_sem.at[5], recv_sem.at[32], zpn_peer(dz, 0))
        else:
            final[z * 8 + pn] = pieces[z, pn]

    wait_bytes(final.at[pl.ds(0, 63)], recv_sem.at[32])
    acc = final[0:8]
    for i in range(1, 8):
        acc = acc + final[i * 8 : (i + 1) * 8]
    even, odd = acc[0] + acc[1] + acc[2] + acc[3], acc[4] + acc[5] + acc[6] + acc[7]
    chosen, is_even = out_row // 2 == out_lane % 8, out_row % 2 == 0
    table = jnp.concatenate(
        [jnp.where(chosen, jnp.where(is_even, even[h : h + 1], odd[h : h + 1]), 0.0) for h in range(2)], axis=1
    )
    place = ones_where(iota((256, 32), 0) // 8 == iota((256, 32), 1), F32)
    out = jnp.dot(table, place, precision=HIGH, preferred_element_type=F32)
    out_ref[...] = (out + out_res).astype(BF16)

    for index, ref in (
        (0, heads.at[pl.ds(0, 7), 0]),
        (1, heads.at[:, pl.ds(0, 7)]),
        (2, parts.at[pl.ds(0, 31)]),
        (3, hidden.at[:, pl.ds(0, 7)]),
        (4, partial.at[:, pl.ds(0, 7)]),
        (5, final.at[pl.ds(0, 63)]),
    ):
        wait_bytes(ref, send_sem.at[index])


def local(
    queries, new_keys, new_values, key_cache, value_cache, lengths, residual, out_weight, norm_gain,
    expert_ids, expert_weights, gate_proj, up_proj, down_proj,
):
    args = (
        key_cache[:, :, 0, :], queries, lengths, new_keys[:, 0, :], new_values[:, 0, :], value_cache[:, :, 0, :],
        out_weight, residual.T, norm_gain, expert_ids.T, expert_weights.T, gate_proj[0], up_proj[0], down_proj[0],
    )
    args = [pltpu.with_memory_space_constraint(a, pltpu.HBM) for a in args]
    held = [pltpu.VMEM(a.shape, a.dtype) for a in args]
    for i in (0, 1, 5):
        held[i] = pltpu.VMEM(args[i].shape[1:], BF16)
    held[2] = pltpu.SMEM((2,), jnp.int32)
    tiles = lambda *lead: pltpu.VMEM((*lead, 16, 128), BF16)
    return pl.pallas_call(
        step,
        out_shape=pltpu.VMEM((16, 32), BF16),
        in_specs=[pl.BlockSpec(memory_space=pl.ANY)] * len(args),
        out_specs=pl.BlockSpec(memory_space=pltpu.VMEM),
        scratch_shapes=held
        + [
            tiles(8, 8), pltpu.VMEM((1024, 128), F32), tiles(32), tiles(8, 8),
            pltpu.VMEM((768, 1024), BF16), pltpu.VMEM((2, 1024, 192), BF16), pltpu.VMEM((768, 128), F32),
            tiles(8, 8), tiles(8, 8), pltpu.VMEM((8, 8, 2, 128), F32), pltpu.VMEM((64, 2, 128), F32),
            pltpu.SemaphoreType.DMA((14,)), pltpu.SemaphoreType.DMA((6,)), pltpu.SemaphoreType.DMA((33,)),
        ],
        compiler_params=pltpu.CompilerParams(
            collective_id=0, has_side_effects=True, vmem_limit_bytes=32 * 1024 * 1024
        ),
    )(*args)


def solution(mesh):
    in_specs = (
        P("wide", "narrow", None),
        P("wide", "narrow", None),
        P("wide", "narrow", None),
        P("wide", None, "narrow", None),
        P("wide", None, "narrow", None),
        P("wide"),
        P(None, "wide"),
        P("wide", "narrow"),
        P(),
        P(),
        P(),
        P("wide", "narrow", None),
        P("wide", "narrow", None),
        P("wide", "narrow", None),
    )
    return jax.shard_map(
        local, mesh=mesh, in_specs=in_specs, out_specs=P(("pool", "narrow"), "wide"), check_vma=False
    )
```

```python
import functools

import jax
import jax.numpy as jnp
from jax import lax
from jax.experimental import pallas as pl
from jax.experimental.pallas import tpu as pltpu
from jax.sharding import PartitionSpec as P

BF16, F32 = jnp.bfloat16, jnp.float32
NT = (((1,), (1,)), ((), ()))
HIGH = lax.Precision.HIGHEST


def iota(shape, axis):
    return lax.broadcasted_iota(jnp.int32, shape, axis)


def ones_where(mask, dtype=BF16):
    return jnp.where(mask, 1.0, 0.0).astype(dtype)


def send(src, dst, send_sem, recv_sem, device):
    pltpu.make_async_remote_copy(
        src_ref=src,
        dst_ref=dst,
        send_sem=send_sem,
        recv_sem=recv_sem,
        device_id=device,
        device_id_type=pl.DeviceIdType.MESH,
    ).start()


def wait_bytes(ref, sem):
    pltpu.make_async_copy(ref, ref, sem).wait()


FAR, NEAR = (4, 3, 5, 2, 6, 1, 7), (1, 7, 2, 6, 3, 5, 4)


def far_offset(i):
    return 4 + (2 * (i % 2) - 1) * ((i + 1) // 2)


def step(
    k_h, q_h, len_h, nk_h, nv_h, v_h, w_h, res_h, gain_h, ids_h, ew_h, gate_h, up_h, down_h,
    out_ref,
    k_v, q_v, len_v, nk_v, nv_v, v_v, w_v, res_v, gain_v, ids_v, ew_v, gate_v, up_v, down_v,
    heads, heads_f, parts, hidden, gu_w, down_w, both, made, partial, pieces, final,
    load_sem, send_sem, recv_sem,
):
    p = lax.axis_index("pool")
    w = lax.axis_index("wide")
    n = lax.axis_index("narrow")
    z, xc = w // 8, w % 8
    pn = p * 4 + n

    loads = [
        (k_h.at[p], k_v), (q_h.at[p], q_v), (len_h, len_v), (nk_h, nk_v), (nv_h, nv_v), (v_h.at[p], v_v),
        (w_h, w_v), (res_h, res_v), (gain_h, gain_v), (ids_h, ids_v), (ew_h, ew_v),
        (gate_h, gate_v), (up_h, up_v), (down_h, down_v),
    ]
    loads = [pltpu.make_async_copy(s, d, load_sem.at[i]) for i, (s, d) in enumerate(loads)]
    for copy in loads[:6]:
        copy.start()

    def at_z(dz):
        return (z + dz) % 8

    def wide_peer(dz, dxc):
        return {"wide": at_z(dz) * 8 + (xc + dxc) % 8}

    def zn_peer(dz, dn):
        return {"wide": at_z(dz) * 8 + xc, "narrow": (n + dn) % 4}

    def zpn_peer(dz, dpn):
        return {"pool": (pn + dpn) % 8 // 4, "wide": at_z(dz) * 8 + xc, "narrow": (pn + dpn) % 4}

    barrier = pltpu.get_barrier_semaphore()
    greeted = [wide_peer(d, 0) for d in FAR] + [zn_peer(0, d) for d in (2, 1, 3)]
    greeted += [wide_peer(0, d) for d in FAR] + [{"pool": 1 - p}]
    for peer in greeted:
        pl.semaphore_signal(barrier, inc=1, device_id=peer, device_id_type=pl.DeviceIdType.MESH)
    for copy in loads[6:]:
        copy.start()

    loads[0].wait()
    loads[1].wait()
    q = q_v[...]
    scale = 128.0**-0.5
    scores = lax.dot_general(q, k_v[...], NT, preferred_element_type=F32) * scale
    for copy in loads[2:6]:
        copy.wait()
    nk = jnp.where(p == 0, nk_v[0:1].astype(F32), nk_v[1:2].astype(F32))
    nv = jnp.where(p == 0, nv_v[0:1].astype(F32), nv_v[1:2].astype(F32))
    self_score = jnp.sum(q.astype(F32) * nk, axis=1, keepdims=True) * scale
    valid = iota((16, 512), 1) < len_v[p]
    scores = jnp.where(valid, scores, -1e30)
    peak = jnp.maximum(jnp.max(scores, axis=1, keepdims=True), self_score)
    weights = jnp.where(valid, jnp.exp(scores - peak), 0.0)
    self_weight = jnp.exp(self_score - peak)
    total = jnp.sum(weights, axis=1, keepdims=True) + self_weight
    probs = (weights / total).astype(BF16)
    self_prob = (self_weight / total).astype(BF16).astype(F32)
    mixed = jnp.dot(probs, v_v[...], preferred_element_type=F32) + self_prob * nv
    heads[z, xc] = mixed.astype(BF16)

    def fan_out(source, send_index, recv_index):
        for i in range(7):
            send(source, source, send_sem.at[send_index], recv_sem.at[recv_index], wide_peer(0, far_offset(i)))

    pl.semaphore_wait(barrier, len(greeted))
    for d in FAR:
        send(heads.at[z, xc], heads.at[z, xc], send_sem.at[0], recv_sem.at[d], wide_peer(d, 0))
    fan_out(heads.at[z, xc], 1, 0)

    for copy in loads[6:]:
        copy.wait()
    gain = gain_v[...].reshape(1, 2048).astype(F32)
    src, dst = iota((256, 256), 0), iota((256, 256), 1)
    perm = ones_where(dst == (src % 32 // 16) * 128 + src // 32 * 16 + src % 16)
    for i, ref in enumerate((gate_v, up_v)):
        for b in range(8):
            cols = slice(b * 256, (b + 1) * 256)
            scaled = (ref[:, cols].astype(F32) * gain[:, cols]).astype(BF16)
            moved = jnp.dot(scaled, perm, preferred_element_type=F32).astype(BF16)
            gu_w[i * 192 : (i + 1) * 192, b * 128 : (b + 1) * 128] = moved[:, :128]
            gu_w[384 + i * 192 : 384 + (i + 1) * 192, b * 128 : (b + 1) * 128] = moved[:, 128:]

    for d in NEAR:
        tile = heads.at[at_z(8 - d), xc]
        wait_bytes(tile, recv_sem.at[d])
        fan_out(tile, 1, 0)

    perm_t = ones_where(src == (dst % 32 // 16) * 128 + dst // 32 * 16 + dst % 16)
    for b in range(8):
        block = down_v[:, b * 256 : (b + 1) * 256]
        moved = lax.dot_general(perm_t, block, NT, preferred_element_type=F32).astype(BF16)
        down_w[0, b * 128 : (b + 1) * 128] = moved[:128]
        down_w[1, b * 128 : (b + 1) * 128] = moved[128:]
    row, lane = iota((128, 128), 0), iota((128, 128), 1)
    pick_low = (lane < 64) & (row == 2 * lane + p)
    pick_high = (lane >= 64) & (row == 2 * (lane - 64) + p)
    res = res_v[...]
    own_res = jnp.dot(res[0:16], ones_where(pick_low), preferred_element_type=F32) + jnp.dot(
        res[16:32], ones_where(pick_high), preferred_element_type=F32
    )
    own_res = jnp.where(n == 0, own_res, 0.0)
    ew = ew_v[...]
    share = jnp.sum(jnp.where(ids_v[...] == w, ew, 0.0), axis=0, keepdims=True)
    share = share / jnp.sum(ew, axis=0, keepdims=True)
    share = jnp.dot(
        jnp.broadcast_to(share, (8, 128)), ones_where(pick_low, F32), precision=HIGH, preferred_element_type=F32
    )[0:1]
    out_row, out_lane = iota((16, 128), 0), iota((16, 128), 1)
    out_res = lax.dot_general(ones_where(out_lane == pn * 16 + out_row), res, NT, preferred_element_type=F32)

    wait_bytes(heads.at[:, pl.ds(0, 7)], recv_sem.at[0])
    heads_f[...] = heads[...].reshape(1024, 128).astype(F32)
    rows = jnp.concatenate([heads_f[pl.ds(g, 64, stride=16), :].astype(BF16) for g in range(16)], axis=1)
    part = lax.dot_general(w_v[...], rows, NT, preferred_element_type=F32)
    part = jnp.concatenate([part[0:16], part[16:32]], axis=1).astype(BF16).astype(F32)

    parts[z * 4 + n] = (part + own_res).astype(BF16)
    for dn in (2, 1, 3, 0):
        for dz in FAR + (0,) if dn else FAR:
            send(parts.at[z * 4 + n], parts.at[z * 4 + n], send_sem.at[2], recv_sem.at[8 + dz], zn_peer(dz, dn))
    for dz in (0,) + NEAR:
        from_z = at_z(8 - dz)
        wait_bytes(parts.at[pl.ds(0, 4 if dz else 3)], recv_sem.at[8 + dz])
        hid = parts[from_z * 4].astype(F32)
        for i in range(1, 4):
            hid = hid + parts[from_z * 4 + i].astype(F32)
        hidden[from_z, xc] = hid.astype(BF16)
        fan_out(hidden.at[from_z, xc], 3, 16 + dz)

    square = jnp.zeros((1, 128), F32)
    for group in ((0,), (1, 7), (2, 6), (3, 5), (4,)):
        tiles, blocks = [], []
        for dz in group:
            from_z = at_z(8 - dz)
            wait_bytes(hidden.at[from_z, pl.ds(0, 7)], recv_sem.at[16 + dz])
            tiles.append(hidden[from_z].reshape(128, 128))
            blocks.append(gu_w[:, pl.ds(pl.multiple_of(from_z * 128, 128), 128)])
        tile = jnp.concatenate(tiles, axis=0)
        term = jnp.dot(jnp.concatenate(blocks, axis=1), tile, preferred_element_type=F32)
        both[...] = term if group == (0,) else both[...] + term
        tile = tile.astype(F32)
        square = square + jnp.sum(tile * tile, axis=0, keepdims=True)
    square = square + pltpu.roll(square, 64, 1)
    inv = lax.rsqrt(square * (1.0 / 2048) + 1e-6)
    act = (both[0:384] + pltpu.roll(both[384:768], 64, 1)) * inv
    gate_vals, up_vals = act[0:192], act[192:384]
    act = gate_vals / (1.0 + jnp.exp(-gate_vals)) * up_vals * share
    act_low, act_high = act.astype(BF16), pltpu.roll(act, 64, 1).astype(BF16)

    for dz in FAR + (0,):
        to_z = at_z(dz)
        rows_w = pl.ds(pl.multiple_of(to_z * 128, 128), 128)
        output = jnp.dot(down_w[0, rows_w], act_low, preferred_element_type=F32) + jnp.dot(
            down_w[1, rows_w], act_high, preferred_element_type=F32
        )
        made[to_z] = output.astype(BF16).reshape(8, 16, 128)

        for i in range(7):
            d = far_offset(i)
            send(
                made.at[to_z, (xc + d) % 8], partial.at[to_z, xc], send_sem.at[4], recv_sem.at[24 + dz],
                wide_peer(0, d),
            )

        partial[to_z, xc] = made[to_z, xc]

    low = out_lane < 64
    repeat = ones_where(iota((128, 16), 0) // 8 == iota((128, 16), 1))
    same_row = lane % 8 == row % 8
    piece_of = ones_where((out_lane // 64 == out_row % 2) & (out_lane % 64 // 8 == out_row // 2))
    for dz in FAR + (0,):
        to_z = at_z(dz)
        wait_bytes(partial.at[to_z, pl.ds(0, 7)], recv_sem.at[24 + dz])
        acc = partial[to_z, 0].astype(F32)
        for i in range(1, 8):
            acc = acc + partial[to_z, i].astype(F32)
        if dz == 0:
            acc = acc + part
        spread = jnp.dot(repeat, acc.astype(BF16), preferred_element_type=F32)
        spread = jnp.where(same_row, spread, 0.0).astype(BF16)
        piece = lax.dot_general(piece_of, spread, NT, preferred_element_type=F32)
        pieces[to_z] = piece.reshape(8, 2, 128)

        for i in range(7):
            d = far_offset(i)
            send(pieces.at[to_z, (pn + d) % 8], final.at[z * 8 + pn], send_sem.at[5], recv_sem.at[32], zpn_peer(dz, d))

        if dz:
            send(pieces.at[to_z, pn], final.at[z * 8 + pn], send_sem.at[5], recv_sem.at[32], zpn_peer(dz, 0))
        else:
            final[z * 8 + pn] = pieces[z, pn]

    wait_bytes(final.at[pl.ds(0, 63)], recv_sem.at[32])
    acc = final[0:8]
    for i in range(1, 8):
        acc = acc + final[i * 8 : (i + 1) * 8]
    even, odd = acc[0] + acc[1] + acc[2] + acc[3], acc[4] + acc[5] + acc[6] + acc[7]
    chosen, is_even = out_row // 2 == out_lane % 8, out_row % 2 == 0
    table = jnp.concatenate(
        [jnp.where(chosen, jnp.where(is_even, even[h : h + 1], odd[h : h + 1]), 0.0) for h in range(2)], axis=1
    )
    place = ones_where(iota((256, 32), 0) // 8 == iota((256, 32), 1), F32)
    out = jnp.dot(table, place, precision=HIGH, preferred_element_type=F32)
    out_ref[...] = (out + out_res).astype(BF16)

    for index, ref in (
        (0, heads.at[pl.ds(0, 7), 0]),
        (1, heads.at[:, pl.ds(0, 7)]),
        (2, parts.at[pl.ds(0, 31)]),
        (3, hidden.at[:, pl.ds(0, 7)]),
        (4, partial.at[:, pl.ds(0, 7)]),
        (5, final.at[pl.ds(0, 63)]),
    ):
        wait_bytes(ref, send_sem.at[index])


def local(
    queries, new_keys, new_values, key_cache, value_cache, lengths, residual, out_weight, norm_gain,
    expert_ids, expert_weights, gate_proj, up_proj, down_proj,
):
    args = (
        key_cache[:, :, 0, :], queries, lengths, new_keys[:, 0, :], new_values[:, 0, :], value_cache[:, :, 0, :],
        out_weight, residual.T, norm_gain, expert_ids.T, expert_weights.T, gate_proj[0], up_proj[0], down_proj[0],
    )
    args = [pltpu.with_memory_space_constraint(a, pltpu.HBM) for a in args]
    held = [pltpu.VMEM(a.shape, a.dtype) for a in args]
    for i in (0, 1, 5):
        held[i] = pltpu.VMEM(args[i].shape[1:], BF16)
    held[2] = pltpu.SMEM((2,), jnp.int32)
    tiles = lambda *lead: pltpu.VMEM((*lead, 16, 128), BF16)
    return pl.pallas_call(
        step,
        out_shape=pltpu.VMEM((16, 32), BF16),
        in_specs=[pl.BlockSpec(memory_space=pl.ANY)] * len(args),
        out_specs=pl.BlockSpec(memory_space=pltpu.VMEM),
        scratch_shapes=held
        + [
            tiles(8, 8), pltpu.VMEM((1024, 128), F32), tiles(32), tiles(8, 8),
            pltpu.VMEM((768, 1024), BF16), pltpu.VMEM((2, 1024, 192), BF16), pltpu.VMEM((768, 128), F32),
            tiles(8, 8), tiles(8, 8), pltpu.VMEM((8, 8, 2, 128), F32), pltpu.VMEM((64, 2, 128), F32),
            pltpu.SemaphoreType.DMA((14,)), pltpu.SemaphoreType.DMA((6,)), pltpu.SemaphoreType.DMA((33,)),
        ],
        compiler_params=pltpu.CompilerParams(
            collective_id=0, has_side_effects=True, vmem_limit_bytes=32 * 1024 * 1024
        ),
    )(*args)


def solution(mesh):
    in_specs = (
        P("wide", "narrow", None),
        P("wide", "narrow", None),
        P("wide", "narrow", None),
        P("wide", None, "narrow", None),
        P("wide", None, "narrow", None),
        P("wide"),
        P(None, "wide"),
        P("wide", "narrow"),
        P(),
        P(),
        P(),
        P("wide", "narrow", None),
        P("wide", "narrow", None),
        P("wide", "narrow", None),
    )
    return jax.shard_map(
        local, mesh=mesh, in_specs=in_specs, out_specs=P(("pool", "narrow"), "wide"), check_vma=False
    )
```
